256 devices in a mesh: sub: 64 (over x, z, core), grp: 4 (over y).
Axes of the slice: x: 4, y: 4, z: 8, core: 2. Of those that a mesh axis runs over, the one named last changes fastest.
Arguments:
- block_map: int32 [4, 64, 5], P('grp', 'sub'), may hold values from 0 to 255, as said below
- interior_inverse: bfloat16 [4, 64, 1029, 1029], P('grp', 'sub'), may hold values from -0.1875 to 0.1875
- coupling: bfloat16 [4, 64, 1029, 640], P('grp', 'sub'), may hold values from -1 to 1
- boundary_block: bfloat16 [4, 64, 5, 128, 128], P('grp', 'sub'), may hold values from -6 to 6
- interface_values: float32 [4, 256, 128], P('grp', 'sub'), may hold values from -0.5 to 0.5
- below_weight: float32 [4, 256, 128], P('grp', 'sub'), may hold values from 1 to 8
- above_weight: float32 [4, 256, 128], P('grp', 'sub'), may hold values from 1 to 8
Outputs:
- schur: float32 [4, 64, 5, 128, 128], P('grp', 'sub')
- assembled: float32 [4, 256, 128, 128], P('grp', 'sub')
- product: float32 [4, 256, 128], P('grp', 'sub')
The draws below stay inside these ranges and needn't reach their ends.
Inputs may be any that keep to these rules, and one draw needn't show every extreme that they name: `block_map`: block g is owned by index g // 4 of sub. The 1 elements of index s of sub name only blocks owned by s or by the indices s + 1, s - 1, s + 2, s - 2, s + 3, s - 3, s + 64 // 2 taken modulo the size of sub; those of any one owner at most 2 times, those of s itself exactly 2 times, those of s + 64 // 2 at least once.
All inputs are finite; a program needn't handle non-finite values.
Results may differ from the reference program's by a relative error of at most 0.0022.
Values sent between devices are 32-bit elements; how exact they have to be, the bound alone decides.
A program may use at most 128 MiB of HBM per device.

```python
import math
import jax
import jax.numpy as jnp
from jax import lax

NI = 1029
BS = 128
NBLK = 5
ELEM_DEV = 1
OWN = 4
CAP = 2
NB = 640
ELEMENTS = 64
G = 256
N_SUB = 64
N_GRP = 4


def draw_block_map(key, part):
    key = jax.random.fold_in(key, 11)
    slots = ELEM_DEV * NBLK
    extra = slots - CAP
    rows = N_GRP * N_SUB
    steps = jnp.array([1, -1, 2, -2, 3, -3, N_SUB // 2], dtype=jnp.int32)

    def one_device(device_key, source):
        first, second, third = jax.random.split(device_key, 3)
        candidates = jnp.arange(CAP * 7 - 1, dtype=jnp.int32)
        shuffled = jax.random.permutation(first, candidates)
        shuffled = shuffled + (shuffled >= 6 * CAP).astype(jnp.int32)
        picked = jnp.concatenate([jnp.full((1,), 6 * CAP, jnp.int32), shuffled[:extra - 1]])
        others = (source + steps[picked // CAP] + N_SUB) % N_SUB
        owners = jnp.concatenate([jnp.full((CAP,), source, jnp.int32), others.astype(jnp.int32)])
        owners = jax.random.permutation(second, owners)
        local = jax.random.randint(third, (slots,), 0, OWN, dtype=jnp.int32)
        return (owners * OWN + local).reshape(ELEM_DEV, NBLK)
    keys = jax.random.split(key, rows)
    sources = jnp.arange(rows, dtype=jnp.int32) % N_SUB
    table = jax.vmap(one_device)(keys, sources)
    return table.reshape(N_GRP, N_SUB * ELEM_DEV, NBLK).astype(jnp.int32)


def level_of(stream_key, dims, pieces, low, high):
    factor_of, own = 1.0, jax.random.fold_in(stream_key, 6)
    for dim, blocks in pieces:
        steps = jnp.exp(jax.random.uniform(jax.random.fold_in(own, dim), (blocks,), jnp.float32, low / len(pieces), high / len(pieces)))
        factor_of = factor_of * jnp.repeat(steps, dims[dim] // blocks).reshape([-1 if axis == dim else 1 for axis in range(len(dims))])
    return factor_of


def bell_draw(stream_key, extent, spread, reach, pieces=(), kind=jnp.bfloat16):
    values = spread * jax.random.normal(stream_key, extent, jnp.float32)
    if pieces:
        values = values * level_of(stream_key, extent, pieces, -0.22, 0.18)
    return jnp.clip(values, -reach, reach).astype(kind)


def setup_inputs(seed: int = 0) -> dict:
    key_list = jax.random.split(jax.random.key(seed), 8)
    block_map = draw_block_map(jax.random.fold_in(key_list[7], 71), 0)
    interior_inverse = bell_draw(key_list[1], (N_GRP, N_SUB, NI, NI), NI ** -0.5, 0.1875, ((0, 4), (1, 64)))
    coupling = bell_draw(key_list[2], (N_GRP, ELEMENTS, NI, NB), (NI ** -0.25), 1.0, ((0, 4), (1, 64)))
    boundary_block = bell_draw(key_list[3], (N_GRP, ELEMENTS, NBLK, BS, BS), 1.0, 6.0, ((0, 4), (1, 64)))
    interface_values = bell_draw(key_list[4], (N_GRP, G, BS), (BS ** -0.5), 0.5, ((0, 4), (1, 64)), jnp.float32)
    below_weight = jnp.clip(jnp.exp(math.log(8.0) - 2.0794415 * jax.random.uniform(key_list[5], (N_GRP, G, BS), jnp.float32) ** level_of(key_list[5], (N_GRP, G, BS), ((0, 4), (1, 64)), -0.2, 0.2)), 1.0, 8.0)
    above_weight = jnp.clip(jnp.exp(math.log(8.0) - 2.0794415 * jax.random.uniform(key_list[6], (N_GRP, G, BS), jnp.float32) ** level_of(key_list[6], (N_GRP, G, BS), ((0, 4), (1, 64)), -0.2, 0.2)), 1.0, 8.0)
    return dict(block_map=block_map, interior_inverse=interior_inverse, coupling=coupling, boundary_block=boundary_block, interface_values=interface_values, below_weight=below_weight, above_weight=above_weight)


def condense(items):
    inverse, coupled, boundary = items
    inverse = inverse.astype(jnp.float32)
    coupled = coupled.astype(jnp.float32)
    solved = jnp.einsum("ij,ejb->eib", inverse, coupled, precision=lax.Precision.HIGHEST).astype(jnp.bfloat16)
    solved = lax.optimization_barrier(solved).astype(jnp.float32)
    elems = coupled.shape[0]
    cview = coupled.reshape(elems, NI, NBLK, BS)
    sview = solved.reshape(elems, NI, NBLK, BS)
    correction = jnp.einsum("eika,eikb->ekab", cview, sview, precision=lax.Precision.HIGHEST)
    return boundary.astype(jnp.float32) - correction


def reference(block_map, interior_inverse, coupling, boundary_block, interface_values, below_weight, above_weight):
    groups = interior_inverse.shape[0]
    subs = interior_inverse.shape[1]
    count = coupling.shape[1]
    flat = (interior_inverse.reshape(groups * subs, NI, NI), coupling.reshape(groups * subs, ELEM_DEV, NI, NB), boundary_block.reshape(groups * subs, ELEM_DEV, NBLK, BS, BS))
    diagonal = lax.map(condense, flat)
    schur = diagonal.reshape(groups, count, NBLK, BS, BS)
    blocks = diagonal.reshape(groups * count * NBLK, BS, BS)
    offsets = (jnp.arange(groups, dtype=jnp.int32) * G)[:, None, None]
    ids = (block_map + offsets).reshape(-1).astype(jnp.int32)
    assembled = jax.ops.segment_sum(blocks, ids, num_segments=groups * G).reshape(groups, G, BS, BS)
    zero_row = jnp.zeros((1, G, BS), jnp.float32)
    lower = jnp.concatenate([zero_row, interface_values[:-1]], axis=0)
    upper = jnp.concatenate([interface_values[1:], zero_row], axis=0)
    applied = jnp.einsum("jgab,jgb->jga", assembled, interface_values, precision=lax.Precision.HIGHEST)
    product = applied - below_weight * lower - above_weight * upper
    return schur, assembled, product
```

```python
import functools

import jax
import jax.numpy as jnp
from jax import lax
from jax.experimental import pallas as pl
from jax.experimental.pallas import tpu as pltpu
from jax.sharding import PartitionSpec as P

MESH = pl.DeviceIdType.MESH
F32 = jnp.float32
TAG = 8


def arrange(block_map, me, size):
    count = block_map.shape[-1]
    ids = [block_map[0, 0, k] for k in range(count)]
    half = lax.rem(me + size // 2, size)
    keys = []
    seen = jnp.int32(0)
    for block in ids:
        owner = block // 4
        is_half = owner == half
        keys.append(jnp.where(owner == me, 3, jnp.where(is_half, jnp.where(seen > 0, 1, 2), 0)))
        seen = seen + is_half.astype(jnp.int32)
    places = []
    for k in range(count):
        place = jnp.int32(0)
        for j in range(count):
            if j < k:
                place = place + (keys[j] <= keys[k]).astype(jnp.int32)
            elif j > k:
                place = place + (keys[j] < keys[k]).astype(jnp.int32)
        places.append(place)
    order, tags = [], []
    for i in range(count):
        pick, tag = jnp.int32(0), jnp.int32(0)
        for k in range(count):
            pick = pick + jnp.where(places[k] == i, k, 0)
            tag = tag + jnp.where(places[k] == i, ids[k], 0)
        order.append(pick)
        tags.append(tag)
    return places, order, tags


def kernel(
    size,
    groups,
    map_hbm,
    inverse_hbm,
    coupling_hbm,
    boundary_hbm,
    values_hbm,
    below_hbm,
    above_hbm,
    schur_ref,
    assembled_ref,
    product_ref,
    block_map,
    inverse,
    coupling,
    boundary,
    values,
    below,
    above,
    lower,
    upper,
    near,
    cross,
    held,
    inbox,
    load_sem,
    send_sem,
    recv_sem,
):
    me, grp = lax.axis_index("sub"), lax.axis_index("grp")
    core = lax.rem(me, 2)
    flip = 1 - 2 * core
    left, right = lax.rem(me + size - 2, size), lax.rem(me + 2, size)
    twin = me + flip
    far = lax.rem(me + size - 3 * flip, size)
    half = lax.rem(me + size // 2, size)
    down, up = lax.rem(grp + groups - 1, groups), lax.rem(grp + 1, groups)

    loads = [
        pltpu.make_async_copy(source, target, load_sem.at[i])
        for i, (source, target) in enumerate(
            (
                (map_hbm, block_map),
                (inverse_hbm.at[0, 0], inverse),
                (boundary_hbm.at[0, 0], boundary),
                (values_hbm.at[0], values),
                (below_hbm.at[0], below),
                (above_hbm.at[0], above),
                *((coupling_hbm.at[0, 0, :, pl.ds(k * 128, 128)], coupling.at[k]) for k in range(5)),
            )
        )
    ]
    for load in loads:
        load.start()

    barrier = pltpu.get_barrier_semaphore()
    partners = [(left, grp), (right, grp), (twin, grp), (far, grp), (half, grp), (me, down), (me, up)]
    for partner in partners:
        pl.semaphore_signal(barrier, inc=1, device_id=partner, device_id_type=MESH)

    def send(index, source, target, device):
        copy = pltpu.make_async_remote_copy(
            src_ref=source,
            dst_ref=target,
            send_sem=send_sem.at[index],
            recv_sem=recv_sem.at[index],
            device_id=device,
            device_id_type=MESH,
        )
        copy.start()
        return copy

    first, second = pl.ds(0, TAG + 128), pl.ds(TAG + 128, 128)

    loads[0].wait()
    places, order, tags = arrange(block_map, me, size)

    def label(target, numbers):
        rows = lax.broadcasted_iota(jnp.int32, (TAG, 128), 0)
        target[0:TAG, :] = jnp.where(rows == 0, numbers[0], numbers[1]).astype(F32)

    label(near, tags[0:2])
    label(cross, (tags[2], tags[1]))

    for load in loads[6:]:
        load.wait()
    loads[1].wait()
    loads[2].wait()

    def condense(picks):
        blocks = [coupling[pick] for pick in picks]
        wide = jnp.concatenate(blocks, axis=1)
        sums = [None] * len(picks)
        for low, high in ((0, 512), (512, inverse.shape[0])):
            solved = jnp.dot(inverse[low:high, :], wide, preferred_element_type=F32).astype(jnp.bfloat16)
            for i, block in enumerate(blocks):
                part = lax.dot_general(
                    block[low:high],
                    solved[:, i * 128 : (i + 1) * 128],
                    (((0,), (0,)), ((), ())),
                    preferred_element_type=F32,
                )
                sums[i] = part if sums[i] is None else sums[i] + part
        return [boundary[pick].astype(F32) - total for pick, total in zip(picks, sums)]

    ahead = condense(order[0:2])
    near[TAG : TAG + 128, :] = ahead[0]
    near[TAG + 128 : TAG + 256, :] = ahead[1]

    pl.semaphore_wait(barrier, len(partners))
    copies = {}
    for part, rows in enumerate((first, second)):
        copies["left", part] = send(part, near.at[rows], inbox.at[1, rows], (left, grp))
        copies["right", part] = send(2 + part, near.at[rows], inbox.at[0, rows], (right, grp))
        copies["twin", part] = send(4 + part, near.at[rows], inbox.at[2, rows], (twin, grp))
    for part, rows in enumerate((first, second)):
        copies["far", part] = send(6 + part, near.at[rows], inbox.at[3, rows], (far, grp))
    copies["half", 1] = send(8, near.at[second], inbox.at[6, second], (half, grp))
    loads[3].wait()
    copies["up"] = send(9, values, lower, (me, up))
    copies["down"] = send(10, values, upper, (me, down))

    behind = condense(order[2:5])
    cross[TAG : TAG + 128, :] = behind[0]
    copies["half", 0] = send(11, cross, inbox.at[6, first], (half, grp))
    for i, block in enumerate(ahead + behind):
        held[i] = block
    for k in range(5):
        schur_ref[0, 0, k] = held[places[k]]

    owned = assembled_ref.shape[1]
    base = me * owned

    def add(block, tag, start=False):
        for q in range(owned):
            term = jnp.where(tag == base + q, block, 0.0)
            assembled_ref[0, q] = term if start else assembled_ref[0, q] + term

    def add_message(slot, part):
        low = TAG + part * 128
        tag = inbox[slot, part : part + 1, :].astype(jnp.int32)
        add(inbox[slot, low : low + 128, :], tag)

    add(held[3], tags[3], start=True)
    add(held[4], tags[4])

    for part, rows in enumerate((first, second)):
        copies["right", part].wait_recv()
        copies["on_left", part] = send(12 + part, inbox.at[0, rows], inbox.at[4, rows], (twin, grp))
        copies["left", part].wait_recv()
        copies["on_right", part] = send(14 + part, inbox.at[1, rows], inbox.at[5, rows], (twin, grp))
    for part in range(2):
        copies["twin", part].wait_recv()
        add_message(2, part)
    for part in range(2):
        add_message(0, part)
        add_message(1, part)
    for part in range(2):
        copies["half", part].wait_recv()
    for part in range(2):
        add_message(6, part)
    for part in range(2):
        copies["on_left", part].wait_recv()
        add_message(4, part)
        copies["on_right", part].wait_recv()
        add_message(5, part)
    for part in range(2):
        copies["far", part].wait_recv()
        add_message(3, part)

    copies["up"].wait_recv()
    copies["down"].wait_recv()
    loads[4].wait()
    loads[5].wait()
    rows = []
    for q in range(owned):
        terms = assembled_ref[0, q] * values[q : q + 1, :]
        rows.append(jnp.sum(terms.T, axis=0, keepdims=True))
    applied = jnp.concatenate(rows, axis=0)
    under = jnp.where(grp > 0, lower[...], 0.0)
    over = jnp.where(grp < groups - 1, upper[...], 0.0)
    product_ref[0] = applied - below[...] * under - above[...] * over
    for copy in copies.values():
        copy.wait_send()


def shards(block_map, interior_inverse, coupling, boundary_block, interface_values, below_weight, above_weight):
    size, groups = lax.axis_size("sub"), lax.axis_size("grp")
    inner = coupling.shape[2]
    count, width = boundary_block.shape[2:4]
    owned = interface_values.shape[1]
    bf16 = jnp.bfloat16
    pair = TAG + 2 * width
    return pl.pallas_call(
        functools.partial(kernel, size, groups),
        out_shape=(
            jax.ShapeDtypeStruct((1, 1, count, width, width), F32),
            jax.ShapeDtypeStruct((1, owned, width, width), F32),
            jax.ShapeDtypeStruct((1, owned, width), F32),
        ),
        in_specs=[pl.BlockSpec(memory_space=pl.ANY)] * 7,
        out_specs=[pl.BlockSpec(memory_space=pltpu.VMEM)] * 3,
        scratch_shapes=[
            pltpu.SMEM(block_map.shape, jnp.int32),
            pltpu.VMEM((inner, inner), bf16),
            pltpu.VMEM((count, inner, width), bf16),
            pltpu.VMEM((count, width, width), bf16),
            pltpu.VMEM((owned, width), F32),
            pltpu.VMEM((owned, width), F32),
            pltpu.VMEM((owned, width), F32),
            pltpu.VMEM((owned, width), F32),
            pltpu.VMEM((owned, width), F32),
            pltpu.VMEM((pair, width), F32),
            pltpu.VMEM((TAG + width, width), F32),
            pltpu.VMEM((count, width, width), F32),
            pltpu.VMEM((7, pair, width), F32),
            pltpu.SemaphoreType.DMA((11,)),
            pltpu.SemaphoreType.DMA((16,)),
            pltpu.SemaphoreType.DMA((16,)),
        ],
        compiler_params=pltpu.CompilerParams(
            collective_id=0, has_side_effects=True, vmem_limit_bytes=56 * 1024 * 1024
        ),
        name="condense_and_assemble",
    )(block_map, interior_inverse, coupling, boundary_block, interface_values, below_weight, above_weight)


def solution(mesh):
    placed = (
        P("grp", "sub", None),
        P("grp", "sub", None, None),
        P("grp", "sub", None, None),
        P("grp", "sub", None, None, None),
        P("grp", "sub", None),
        P("grp", "sub", None),
        P("grp", "sub", None),
    )
    return jax.shard_map(
        shards,
        mesh=mesh,
        in_specs=placed,
        out_specs=(
            P("grp", "sub", None, None, None),
            P("grp", "sub", None, None),
            P("grp", "sub", None),
        ),
        check_vma=False,
    )
```

```python
import functools

import jax
import jax.numpy as jnp
from jax import lax
from jax.experimental import pallas as pl
from jax.experimental.pallas import tpu as pltpu
from jax.sharding import PartitionSpec as P

MESH = pl.DeviceIdType.MESH
F32 = jnp.float32
TAG = 8


def arrange(block_map, me, size):
    count = block_map.shape[-1]
    ids = [block_map[0, 0, k] for k in range(count)]
    half = lax.rem(me + size // 2, size)
    keys = []
    seen = jnp.int32(0)
    for block in ids:
        owner = block // 4
        is_half = owner == half
        keys.append(jnp.where(owner == me, 3, jnp.where(is_half, jnp.where(seen > 0, 1, 2), 0)))
        seen = seen + is_half.astype(jnp.int32)
    places = []
    for k in range(count):
        place = jnp.int32(0)
        for j in range(count):
            if j < k:
                place = place + (keys[j] <= keys[k]).astype(jnp.int32)
            elif j > k:
                place = place + (keys[j] < keys[k]).astype(jnp.int32)
        places.append(place)
    order, tags = [], []
    for i in range(count):
        pick, tag = jnp.int32(0), jnp.int32(0)
        for k in range(count):
            pick = pick + jnp.where(places[k] == i, k, 0)
            tag = tag + jnp.where(places[k] == i, ids[k], 0)
        order.append(pick)
        tags.append(tag)
    return places, order, tags


def kernel(
    size,
    groups,
    map_hbm,
    inverse_hbm,
    coupling_hbm,
    boundary_hbm,
    values_hbm,
    below_hbm,
    above_hbm,
    schur_ref,
    assembled_ref,
    product_ref,
    block_map,
    inverse,
    coupling,
    boundary,
    values,
    below,
    above,
    lower,
    upper,
    near,
    cross,
    held,
    inbox,
    load_sem,
    send_sem,
    recv_sem,
):
    me, grp = lax.axis_index("sub"), lax.axis_index("grp")
    core = lax.rem(me, 2)
    step = 2 * core - 1
    twin = lax.rem(me + size - step, size)
    outer, inner = lax.rem(me + size + 2 * step, size), lax.rem(me + size - 2 * step, size)
    beyond = lax.rem(me + size + step, size)
    half = lax.rem(me + size // 2, size)
    down, up = lax.rem(grp + groups - 1, groups), lax.rem(grp + 1, groups)

    loads = [
        pltpu.make_async_copy(source, target, load_sem.at[i])
        for i, (source, target) in enumerate(
            (
                (map_hbm, block_map),
                (inverse_hbm.at[0, 0], inverse),
                (boundary_hbm.at[0, 0], boundary),
                (values_hbm.at[0], values),
                (below_hbm.at[0], below),
                (above_hbm.at[0], above),
                *((coupling_hbm.at[0, 0, :, pl.ds(k * 128, 128)], coupling.at[k]) for k in range(5)),
            )
        )
    ]
    for load in loads:
        load.start()

    barrier = pltpu.get_barrier_semaphore()
    partners = [(outer, grp), (inner, grp), (twin, grp), (beyond, grp), (half, grp), (me, down), (me, up)]
    for partner in partners:
        pl.semaphore_signal(barrier, inc=1, device_id=partner, device_id_type=MESH)

    def send(index, source, target, device):
        copy = pltpu.make_async_remote_copy(
            src_ref=source,
            dst_ref=target,
            send_sem=send_sem.at[index],
            recv_sem=recv_sem.at[index],
            device_id=device,
            device_id_type=MESH,
        )
        copy.start()
        return copy

    first, second = pl.ds(0, TAG + 128), pl.ds(TAG + 128, 128)

    loads[0].wait()
    places, order, tags = arrange(block_map, me, size)

    def label(target, numbers):
        rows = lax.broadcasted_iota(jnp.int32, (TAG, 128), 0)
        target[0:TAG, :] = jnp.where(rows == 0, numbers[0], numbers[1]).astype(F32)

    label(near, tags[0:2])
    label(cross, (tags[2], tags[1]))

    for load in loads[6:]:
        load.wait()
    loads[1].wait()
    loads[2].wait()

    def condense(picks):
        blocks = [coupling[pick] for pick in picks]
        wide = jnp.concatenate(blocks, axis=1)
        sums = [None] * len(picks)
        for low, high in ((0, 512), (512, inverse.shape[0])):
            solved = jnp.dot(inverse[low:high, :], wide, preferred_element_type=F32).astype(jnp.bfloat16)
            for i, block in enumerate(blocks):
                part = lax.dot_general(
                    block[low:high],
                    solved[:, i * 128 : (i + 1) * 128],
                    (((0,), (0,)), ((), ())),
                    preferred_element_type=F32,
                )
                sums[i] = part if sums[i] is None else sums[i] + part
        return [boundary[pick].astype(F32) - total for pick, total in zip(picks, sums)]

    ahead = condense(order[0:2])
    near[TAG : TAG + 128, :] = ahead[0]
    near[TAG + 128 : TAG + 256, :] = ahead[1]

    pl.semaphore_wait(barrier, len(partners))
    copies = {}
    for part, rows in enumerate((first, second)):
        copies["outer", part] = send(part, near.at[rows], inbox.at[0, rows], (outer, grp))
        copies["inner", part] = send(2 + part, near.at[rows], inbox.at[1, rows], (inner, grp))
    for part, rows in enumerate((first, second)):
        copies["twin", part] = send(4 + part, near.at[rows], inbox.at[2, rows], (twin, grp))
    copies["half", 1] = send(8, near.at[second], inbox.at[6, second], (half, grp))
    loads[3].wait()
    copies["up"] = send(9, values, lower, (me, up))
    copies["down"] = send(10, values, upper, (me, down))

    behind = condense(order[2:5])
    cross[TAG : TAG + 128, :] = behind[0]
    copies["half", 0] = send(11, cross, inbox.at[6, first], (half, grp))
    for i, block in enumerate(ahead + behind):
        held[i] = block
    for k in range(5):
        schur_ref[k] = held[places[k]]

    owned = assembled_ref.shape[0]
    base = me * owned

    def add(block, tag, start=False):
        for q in range(owned):
            term = jnp.where(tag == base + q, block, 0.0)
            assembled_ref[q] = term if start else assembled_ref[q] + term

    def add_message(slot, part):
        low = TAG + part * 128
        tag = inbox[slot, part : part + 1, :].astype(jnp.int32)
        add(inbox[slot, low : low + 128, :], tag)

    add(held[3], tags[3], start=True)
    add(held[4], tags[4])

    for part, rows in enumerate((first, second)):
        copies["outer", part].wait_recv()
        copies["far", part] = send(6 + part, inbox.at[0, rows], inbox.at[3, rows], (beyond, grp))
        copies["on_outer", part] = send(12 + part, inbox.at[0, rows], inbox.at[4, rows], (twin, grp))
        copies["inner", part].wait_recv()
        copies["on_inner", part] = send(14 + part, inbox.at[1, rows], inbox.at[5, rows], (twin, grp))
    for part in range(2):
        copies["twin", part].wait_recv()
        add_message(2, part)
    for part in range(2):
        add_message(0, part)
        add_message(1, part)
    for part in range(2):
        copies["half", part].wait_recv()
    for part in range(2):
        add_message(6, part)
    for part in range(2):
        copies["on_outer", part].wait_recv()
        add_message(4, part)
        copies["on_inner", part].wait_recv()
        add_message(5, part)
    for part in range(2):
        copies["far", part].wait_recv()
        add_message(3, part)

    copies["up"].wait_recv()
    copies["down"].wait_recv()
    loads[4].wait()
    loads[5].wait()
    rows = []
    for q in range(owned):
        terms = assembled_ref[q] * values[q : q + 1, :]
        rows.append(jnp.sum(terms.T, axis=0, keepdims=True))
    applied = jnp.concatenate(rows, axis=0)
    under = jnp.where(grp > 0, lower[...], 0.0)
    over = jnp.where(grp < groups - 1, upper[...], 0.0)
    product_ref[...] = applied - below[...] * under - above[...] * over
    for copy in copies.values():
        copy.wait_send()


def write_out(schur, assembled, product, schur_hbm, assembled_hbm, product_hbm, sem):
    copies = [
        pltpu.make_async_copy(source, target, sem.at[i])
        for i, (source, target) in enumerate(
            ((schur, schur_hbm.at[0, 0]), (assembled, assembled_hbm.at[0]), (product, product_hbm.at[0]))
        )
    ]
    for copy in copies:
        copy.start()
    for copy in copies:
        copy.wait()


def shards(block_map, interior_inverse, coupling, boundary_block, interface_values, below_weight, above_weight):
    size, groups = lax.axis_size("sub"), lax.axis_size("grp")
    inner = coupling.shape[2]
    count, width = boundary_block.shape[2:4]
    owned = interface_values.shape[1]
    bf16 = jnp.bfloat16
    pair = TAG + 2 * width
    results = pl.pallas_call(
        functools.partial(kernel, size, groups),
        out_shape=(
            pltpu.VMEM((count, width, width), F32),
            pltpu.VMEM((owned, width, width), F32),
            pltpu.VMEM((owned, width), F32),
        ),
        in_specs=[pl.BlockSpec(memory_space=pl.ANY)] * 7,
        out_specs=[pl.BlockSpec(memory_space=pltpu.VMEM)] * 3,
        scratch_shapes=[
            pltpu.SMEM(block_map.shape, jnp.int32),
            pltpu.VMEM((inner, inner), bf16),
            pltpu.VMEM((count, inner, width), bf16),
            pltpu.VMEM((count, width, width), bf16),
            pltpu.VMEM((owned, width), F32),
            pltpu.VMEM((owned, width), F32),
            pltpu.VMEM((owned, width), F32),
            pltpu.VMEM((owned, width), F32),
            pltpu.VMEM((owned, width), F32),
            pltpu.VMEM((pair, width), F32),
            pltpu.VMEM((TAG + width, width), F32),
            pltpu.VMEM((count, width, width), F32),
            pltpu.VMEM((7, pair, width), F32),
            pltpu.SemaphoreType.DMA((11,)),
            pltpu.SemaphoreType.DMA((16,)),
            pltpu.SemaphoreType.DMA((16,)),
        ],
        compiler_params=pltpu.CompilerParams(
            collective_id=0, has_side_effects=True, vmem_limit_bytes=56 * 1024 * 1024
        ),
        name="condense_and_assemble",
    )(block_map, interior_inverse, coupling, boundary_block, interface_values, below_weight, above_weight)

    results = [pltpu.with_memory_space_constraint(x, pltpu.VMEM) for x in results]
    return pl.pallas_call(
        write_out,
        out_shape=(
            jax.ShapeDtypeStruct((1, 1, count, width, width), F32),
            jax.ShapeDtypeStruct((1, owned, width, width), F32),
            jax.ShapeDtypeStruct((1, owned, width), F32),
        ),
        in_specs=[pl.BlockSpec(memory_space=pltpu.VMEM)] * 3,
        out_specs=[pl.BlockSpec(memory_space=pl.ANY)] * 3,
        scratch_shapes=[pltpu.SemaphoreType.DMA((3,))],
        name="write_out",
    )(*results)


def solution(mesh):
    placed = (
        P("grp", "sub", None),
        P("grp", "sub", None, None),
        P("grp", "sub", None, None),
        P("grp", "sub", None, None, None),
        P("grp", "sub", None),
        P("grp", "sub", None),
        P("grp", "sub", None),
    )
    return jax.shard_map(
        shards,
        mesh=mesh,
        in_specs=placed,
        out_specs=(
            P("grp", "sub", None, None, None),
            P("grp", "sub", None, None),
            P("grp", "sub", None),
        ),
        check_vma=False,
    )
```

```python
import functools

import jax
import jax.numpy as jnp
from jax import lax
from jax.experimental import pallas as pl
from jax.experimental.pallas import tpu as pltpu
from jax.sharding import PartitionSpec as P

MESH = pl.DeviceIdType.MESH
F32 = jnp.float32
PLANES = 8
TAG = 8


def arrange(block_map, me, size):
    count = block_map.shape[-1]
    ids = [block_map[0, 0, k] for k in range(count)]
    half = lax.rem(me + size // 2, size)
    keys = []
    seen = jnp.int32(0)
    for block in ids:
        owner = block // 4
        is_half = owner == half
        keys.append(jnp.where(owner == me, 3, jnp.where(is_half, jnp.where(seen > 0, 1, 2), 0)))
        seen = seen + is_half.astype(jnp.int32)
    places = []
    for k in range(count):
        place = jnp.int32(0)
        for j in range(count):
            if j < k:
                place = place + (keys[j] <= keys[k]).astype(jnp.int32)
            elif j > k:
                place = place + (keys[j] < keys[k]).astype(jnp.int32)
        places.append(place)
    order, tags = [], []
    for i in range(count):
        pick, tag = jnp.int32(0), jnp.int32(0)
        for k in range(count):
            pick = pick + jnp.where(places[k] == i, k, 0)
            tag = tag + jnp.where(places[k] == i, ids[k], 0)
        order.append(pick)
        tags.append(tag)
    return places, order, tags


def kernel(
    size,
    groups,
    map_hbm,
    inverse_hbm,
    coupling_hbm,
    boundary_hbm,
    values_hbm,
    below_hbm,
    above_hbm,
    schur_ref,
    assembled_ref,
    product_ref,
    block_map,
    inverse,
    coupling,
    boundary,
    values,
    below,
    above,
    lower,
    upper,
    near,
    cross,
    held,
    inbox,
    load_sem,
    send_sem,
    recv_sem,
    ready,
):
    me, grp = lax.axis_index("sub"), lax.axis_index("grp")
    core = lax.rem(me, 2)
    step = 2 * core - 1
    twin = lax.rem(me + size - step, size)
    outer = lax.rem(me + size + 2 * step, size)
    behind = lax.rem(me + size - 2 * step, size)
    inner = lax.rem(me + size - 3 * step, size)
    beyond = lax.rem(me + size + step, size)
    half = lax.rem(me + size // 2, size)
    plane = lax.rem(me // 2, PLANES)
    bottom, top = plane == 0, plane == PLANES - 1
    odd = core == 1
    bottom_odd, bottom_even = jnp.logical_and(bottom, odd), jnp.logical_and(bottom, core == 0)
    top_odd, top_even = jnp.logical_and(top, odd), jnp.logical_and(top, core == 0)
    down, up = lax.rem(grp + groups - 1, groups), lax.rem(grp + 1, groups)

    loads = [
        pltpu.make_async_copy(source, target, load_sem.at[i])
        for i, (source, target) in enumerate(
            (
                (map_hbm, block_map),
                (inverse_hbm.at[0, 0], inverse),
                (boundary_hbm.at[0, 0], boundary),
                (values_hbm.at[0], values),
                (below_hbm.at[0], below),
                (above_hbm.at[0], above),
                *((coupling_hbm.at[0, 0, :, pl.ds(k * 128, 128)], coupling.at[k]) for k in range(5)),
            )
        )
    ]
    for load in loads:
        load.start()

    barrier = pltpu.get_barrier_semaphore()
    def signal(semaphore, *peers):
        for peer in peers:
            pl.semaphore_signal(semaphore, inc=1, device_id=peer, device_id_type=MESH)

    signal(barrier, (twin, grp), (half, grp), (me, down), (me, up))

    @pl.when(jnp.logical_not(top_odd))
    def _():
        signal(barrier, (outer, grp), (beyond, grp))

    @pl.when(jnp.logical_not(top_even))
    def _():
        signal(barrier, (behind, grp), (inner, grp))

    def describe(index, source, target, device):
        return pltpu.make_async_remote_copy(
            src_ref=source,
            dst_ref=target,
            send_sem=send_sem.at[index],
            recv_sem=recv_sem.at[index],
            device_id=device,
            device_id_type=MESH,
        )

    def send(*args):
        copy = describe(*args)
        copy.start()
        return copy

    first, second = pl.ds(0, TAG + 128), pl.ds(TAG + 128, 128)

    loads[0].wait()
    places, order, tags = arrange(block_map, me, size)

    def label(target, numbers):
        rows = lax.broadcasted_iota(jnp.int32, (TAG, 128), 0)
        target[0:TAG, :] = jnp.where(rows == 0, numbers[0], numbers[1]).astype(F32)

    label(near, tags[0:2])
    label(cross, (tags[2], tags[1]))

    for load in loads[6:]:
        load.wait()
    loads[1].wait()
    loads[2].wait()

    def condense(picks):
        blocks = [coupling[pick] for pick in picks]
        wide = jnp.concatenate(blocks, axis=1)
        sums = [None] * len(picks)
        for low, high in ((0, 512), (512, inverse.shape[0])):
            solved = jnp.dot(inverse[low:high, :], wide, preferred_element_type=F32).astype(jnp.bfloat16)
            for i, block in enumerate(blocks):
                part = lax.dot_general(
                    block[low:high],
                    solved[:, i * 128 : (i + 1) * 128],
                    (((0,), (0,)), ((), ())),
                    preferred_element_type=F32,
                )
                sums[i] = part if sums[i] is None else sums[i] + part
        return [boundary[pick].astype(F32) - total for pick, total in zip(picks, sums)]

    ahead = condense(order[0:2])
    near[TAG : TAG + 128, :] = ahead[0]
    near[TAG + 128 : TAG + 256, :] = ahead[1]

    pl.semaphore_wait(barrier, 8 - 2 * bottom.astype(jnp.int32))

    @pl.when(top_odd)
    def _():
        signal(ready, (outer, grp), (beyond, grp))

    @pl.when(top_even)
    def _():
        signal(ready, (behind, grp), (inner, grp))

    copies = {}
    for part, rows in enumerate((first, second)):
        copies["outer", part] = describe(part, near.at[rows], inbox.at[0, rows], (outer, grp))
        copies["inner", part] = describe(2 + part, near.at[rows], inbox.at[1, rows], (inner, grp))
        pl.when(jnp.logical_not(bottom_even))(copies["outer", part].start)
        pl.when(jnp.logical_not(bottom_odd))(copies["inner", part].start)
    for part, rows in enumerate((first, second)):
        copies["twin", part] = send(4 + part, near.at[rows], inbox.at[2, rows], (twin, grp))
    copies["half", 1] = send(8, near.at[second], inbox.at[6, second], (half, grp))
    loads[3].wait()
    copies["up"] = send(9, values, lower, (me, up))
    copies["down"] = send(10, values, upper, (me, down))

    later = condense(order[2:5])
    cross[TAG : TAG + 128, :] = later[0]
    copies["half", 0] = send(11, cross, inbox.at[6, first], (half, grp))

    @pl.when(bottom)
    def _():
        pl.semaphore_wait(ready, 2)

    for part in range(2):
        pl.when(bottom_even)(copies["outer", part].start)
        pl.when(bottom_odd)(copies["inner", part].start)
    for i, block in enumerate(ahead + later):
        held[i] = block
    for k in range(5):
        schur_ref[k] = held[places[k]]

    owned = assembled_ref.shape[0]
    base = me * owned

    def add(block, tag, start=False):
        for q in range(owned):
            term = jnp.where(tag == base + q, block, 0.0)
            assembled_ref[q] = term if start else assembled_ref[q] + term

    def add_message(slot, part):
        low = TAG + part * 128
        tag = inbox[slot, part : part + 1, :].astype(jnp.int32)
        add(inbox[slot, low : low + 128, :], tag)

    add(held[3], tags[3], start=True)
    add(held[4], tags[4])

    for part, rows in enumerate((first, second)):
        copies["outer", part].wait_recv()
        copies["far", part] = send(6 + part, inbox.at[0, rows], inbox.at[3, rows], (beyond, grp))
        copies["on_outer", part] = send(12 + part, inbox.at[0, rows], inbox.at[4, rows], (twin, grp))
        copies["inner", part].wait_recv()
        copies["on_inner", part] = send(14 + part, inbox.at[1, rows], inbox.at[5, rows], (twin, grp))
    for part in range(2):
        copies["twin", part].wait_recv()
        add_message(2, part)
    for part in range(2):
        add_message(0, part)
        add_message(1, part)
    for part in range(2):
        copies["half", part].wait_recv()
    for part in range(2):
        add_message(6, part)
    for part in range(2):
        copies["on_outer", part].wait_recv()
        add_message(4, part)
        copies["on_inner", part].wait_recv()
        add_message(5, part)
    for part in range(2):
        copies["far", part].wait_recv()
        add_message(3, part)

    copies["up"].wait_recv()
    copies["down"].wait_recv()
    loads[4].wait()
    loads[5].wait()
    rows = []
    for q in range(owned):
        terms = assembled_ref[q] * values[q : q + 1, :]
        rows.append(jnp.sum(terms.T, axis=0, keepdims=True))
    applied = jnp.concatenate(rows, axis=0)
    under = jnp.where(grp > 0, lower[...], 0.0)
    over = jnp.where(grp < groups - 1, upper[...], 0.0)
    product_ref[...] = applied - below[...] * under - above[...] * over
    for copy in copies.values():
        copy.wait_send()


def write_out(schur, assembled, product, schur_hbm, assembled_hbm, product_hbm, sem):
    copies = [
        pltpu.make_async_copy(source, target, sem.at[i])
        for i, (source, target) in enumerate(
            ((schur, schur_hbm.at[0, 0]), (assembled, assembled_hbm.at[0]), (product, product_hbm.at[0]))
        )
    ]
    for copy in copies:
        copy.start()
    for copy in copies:
        copy.wait()


def shards(block_map, interior_inverse, coupling, boundary_block, interface_values, below_weight, above_weight):
    size, groups = lax.axis_size("sub"), lax.axis_size("grp")
    inner = coupling.shape[2]
    count, width = boundary_block.shape[2:4]
    owned = interface_values.shape[1]
    bf16 = jnp.bfloat16
    pair = TAG + 2 * width
    results = pl.pallas_call(
        functools.partial(kernel, size, groups),
        out_shape=(
            pltpu.VMEM((count, width, width), F32),
            pltpu.VMEM((owned, width, width), F32),
            pltpu.VMEM((owned, width), F32),
        ),
        in_specs=[pl.BlockSpec(memory_space=pl.ANY)] * 7,
        out_specs=[pl.BlockSpec(memory_space=pltpu.VMEM)] * 3,
        scratch_shapes=[
            pltpu.SMEM(block_map.shape, jnp.int32),
            pltpu.VMEM((inner, inner), bf16),
            pltpu.VMEM((count, inner, width), bf16),
            pltpu.VMEM((count, width, width), bf16),
            pltpu.VMEM((owned, width), F32),
            pltpu.VMEM((owned, width), F32),
            pltpu.VMEM((owned, width), F32),
            pltpu.VMEM((owned, width), F32),
            pltpu.VMEM((owned, width), F32),
            pltpu.VMEM((pair, width), F32),
            pltpu.VMEM((TAG + width, width), F32),
            pltpu.VMEM((count, width, width), F32),
            pltpu.VMEM((7, pair, width), F32),
            pltpu.SemaphoreType.DMA((11,)),
            pltpu.SemaphoreType.DMA((16,)),
            pltpu.SemaphoreType.DMA((16,)),
            pltpu.SemaphoreType.REGULAR,
        ],
        compiler_params=pltpu.CompilerParams(
            collective_id=0, has_side_effects=True, vmem_limit_bytes=56 * 1024 * 1024
        ),
        name="condense_and_assemble",
    )(block_map, interior_inverse, coupling, boundary_block, interface_values, below_weight, above_weight)

    results = [pltpu.with_memory_space_constraint(x, pltpu.VMEM) for x in results]
    return pl.pallas_call(
        write_out,
        out_shape=(
            jax.ShapeDtypeStruct((1, 1, count, width, width), F32),
            jax.ShapeDtypeStruct((1, owned, width, width), F32),
            jax.ShapeDtypeStruct((1, owned, width), F32),
        ),
        in_specs=[pl.BlockSpec(memory_space=pltpu.VMEM)] * 3,
        out_specs=[pl.BlockSpec(memory_space=pl.ANY)] * 3,
        scratch_shapes=[pltpu.SemaphoreType.DMA((3,))],
        name="write_out",
    )(*results)


def solution(mesh):
    placed = (
        P("grp", "sub", None),
        P("grp", "sub", None, None),
        P("grp", "sub", None, None),
        P("grp", "sub", None, None, None),
        P("grp", "sub", None),
        P("grp", "sub", None),
        P("grp", "sub", None),
    )
    return jax.shard_map(
        shards,
        mesh=mesh,
        in_specs=placed,
        out_specs=(
            P("grp", "sub", None, None, None),
            P("grp", "sub", None, None),
            P("grp", "sub", None),
        ),
        check_vma=False,
    )
```

```python
import functools

import jax
import jax.numpy as jnp
from jax import lax
from jax.experimental import pallas as pl
from jax.experimental.pallas import tpu as pltpu
from jax.sharding import PartitionSpec as P

MESH = pl.DeviceIdType.MESH
F32 = jnp.float32
PLANES = 8
TAG = 8


def arrange(block_map, me, size):
    count = block_map.shape[-1]
    ids = [block_map[0, 0, k] for k in range(count)]
    half = lax.rem(me + size // 2, size)
    keys = []
    seen = jnp.int32(0)
    for block in ids:
        owner = block // 4
        is_half = owner == half
        keys.append(jnp.where(owner == me, 3, jnp.where(is_half, jnp.where(seen > 0, 1, 2), 0)))
        seen = seen + is_half.astype(jnp.int32)
    places = []
    for k in range(count):
        place = jnp.int32(0)
        for j in range(count):
            if j < k:
                place = place + (keys[j] <= keys[k]).astype(jnp.int32)
            elif j > k:
                place = place + (keys[j] < keys[k]).astype(jnp.int32)
        places.append(place)
    order, tags = [], []
    for i in range(count):
        pick, tag = jnp.int32(0), jnp.int32(0)
        for k in range(count):
            pick = pick + jnp.where(places[k] == i, k, 0)
            tag = tag + jnp.where(places[k] == i, ids[k], 0)
        order.append(pick)
        tags.append(tag)
    return places, order, tags


def kernel(
    size,
    groups,
    map_hbm,
    inverse_hbm,
    coupling_hbm,
    boundary_hbm,
    values_hbm,
    below_hbm,
    above_hbm,
    schur_ref,
    assembled_ref,
    product_ref,
    block_map,
    inverse,
    coupling,
    boundary,
    values,
    below,
    above,
    lower,
    upper,
    near,
    cross,
    held,
    inbox,
    load_sem,
    send_sem,
    recv_sem,
    ready,
):
    me, grp = lax.axis_index("sub"), lax.axis_index("grp")
    core = lax.rem(me, 2)
    step = 2 * core - 1
    twin = lax.rem(me + size - step, size)
    outer = lax.rem(me + size + 2 * step, size)
    behind = lax.rem(me + size - 2 * step, size)
    inner = lax.rem(me + size - 3 * step, size)
    beyond = lax.rem(me + size + step, size)
    half = lax.rem(me + size // 2, size)
    plane = lax.rem(me // 2, PLANES)
    bottom, top = plane == 0, plane == PLANES - 1
    odd = core == 1
    bottom_odd, bottom_even = jnp.logical_and(bottom, odd), jnp.logical_and(bottom, core == 0)
    top_odd, top_even = jnp.logical_and(top, odd), jnp.logical_and(top, core == 0)
    down, up = lax.rem(grp + groups - 1, groups), lax.rem(grp + 1, groups)

    loads = [
        pltpu.make_async_copy(source, target, load_sem.at[i])
        for i, (source, target) in enumerate(
            (
                (map_hbm, block_map),
                (inverse_hbm.at[0, 0], inverse),
                (boundary_hbm.at[0, 0], boundary),
                (values_hbm.at[0], values),
                (below_hbm.at[0], below),
                (above_hbm.at[0], above),
                *((coupling_hbm.at[0, 0, :, pl.ds(k * 128, 128)], coupling.at[k]) for k in range(5)),
            )
        )
    ]
    for load in loads:
        load.start()

    barrier = pltpu.get_barrier_semaphore()
    def signal(semaphore, *peers):
        for peer in peers:
            pl.semaphore_signal(semaphore, inc=1, device_id=peer, device_id_type=MESH)

    signal(barrier, (twin, grp), (half, grp), (me, down), (me, up))

    @pl.when(jnp.logical_not(top_odd))
    def _():
        signal(barrier, (outer, grp), (beyond, grp))

    @pl.when(jnp.logical_not(top_even))
    def _():
        signal(barrier, (behind, grp), (inner, grp))

    def describe(index, source, target, device):
        return pltpu.make_async_remote_copy(
            src_ref=source,
            dst_ref=target,
            send_sem=send_sem.at[index],
            recv_sem=recv_sem.at[index],
            device_id=device,
            device_id_type=MESH,
        )

    def send(*args):
        copy = describe(*args)
        copy.start()
        return copy

    first, second = pl.ds(0, TAG + 128), pl.ds(TAG + 128, 128)

    loads[0].wait()
    places, order, tags = arrange(block_map, me, size)

    def label(target, numbers):
        rows = lax.broadcasted_iota(jnp.int32, (TAG, 128), 0)
        target[0:TAG, :] = jnp.where(rows == 0, numbers[0], numbers[1]).astype(F32)

    label(near, tags[0:2])
    label(cross, (tags[2], tags[1]))

    for load in loads[6:]:
        load.wait()
    loads[1].wait()
    loads[2].wait()

    def condense(picks):
        blocks = [coupling[pick] for pick in picks]
        wide = jnp.concatenate(blocks, axis=1)
        sums = [None] * len(picks)
        for low, high in ((0, 512), (512, inverse.shape[0])):
            solved = jnp.dot(inverse[low:high, :], wide, preferred_element_type=F32).astype(jnp.bfloat16)
            for i, block in enumerate(blocks):
                part = lax.dot_general(
                    block[low:high],
                    solved[:, i * 128 : (i + 1) * 128],
                    (((0,), (0,)), ((), ())),
                    preferred_element_type=F32,
                )
                sums[i] = part if sums[i] is None else sums[i] + part
        return [boundary[pick].astype(F32) - total for pick, total in zip(picks, sums)]

    ahead = condense(order[0:2])
    near[TAG : TAG + 128, :] = ahead[0]
    near[TAG + 128 : TAG + 256, :] = ahead[1]

    pl.semaphore_wait(barrier, 8 - 2 * bottom.astype(jnp.int32))

    copies = {}
    for part, rows in enumerate((first, second)):
        copies["outer", part] = describe(part, near.at[rows], inbox.at[0, rows], (outer, grp))
        copies["inner", part] = describe(2 + part, near.at[rows], inbox.at[1, rows], (inner, grp))
        pl.when(jnp.logical_not(bottom_even))(copies["outer", part].start)
        pl.when(top)(copies["inner", part].start)

    @pl.when(top_odd)
    def _():
        signal(ready, (outer, grp), (beyond, grp))

    @pl.when(top_even)
    def _():
        signal(ready, (behind, grp), (inner, grp))

    for part, rows in enumerate((first, second)):
        copies["twin", part] = send(4 + part, near.at[rows], inbox.at[2, rows], (twin, grp))
    copies["half", 1] = send(8, near.at[second], inbox.at[6, second], (half, grp))
    loads[3].wait()
    copies["up"] = send(9, values, lower, (me, up))
    copies["down"] = send(10, values, upper, (me, down))

    later = condense(order[2:3])
    cross[TAG : TAG + 128, :] = later[0]
    copies["half", 0] = send(11, cross, inbox.at[6, first], (half, grp))
    for part in range(2):
        pl.when(jnp.logical_not(jnp.logical_or(top, bottom_odd)))(copies["inner", part].start)
    later += condense(order[3:5])

    @pl.when(bottom)
    def _():
        pl.semaphore_wait(ready, 2)

    for part in range(2):
        pl.when(bottom_even)(copies["outer", part].start)
        pl.when(bottom_odd)(copies["inner", part].start)
    for i, block in enumerate(ahead + later):
        held[i] = block
    for k in range(5):
        schur_ref[k] = held[places[k]]

    owned = assembled_ref.shape[0]
    base = me * owned

    def add(block, tag, start=False):
        for q in range(owned):
            term = jnp.where(tag == base + q, block, 0.0)
            assembled_ref[q] = term if start else assembled_ref[q] + term

    def add_message(slot, part):
        low = TAG + part * 128
        tag = inbox[slot, part : part + 1, :].astype(jnp.int32)
        add(inbox[slot, low : low + 128, :], tag)

    add(held[3], tags[3], start=True)
    add(held[4], tags[4])

    for part in range(2):
        copies["twin", part].wait_recv()
        add_message(2, part)
    for part, rows in enumerate((first, second)):
        copies["outer", part].wait_recv()
        copies["on_outer", part] = send(12 + part, inbox.at[0, rows], inbox.at[4, rows], (twin, grp))
        copies["far", part] = send(6 + part, inbox.at[0, rows], inbox.at[3, rows], (beyond, grp))
    for part, rows in enumerate((first, second)):
        copies["inner", part].wait_recv()
        copies["on_inner", part] = send(14 + part, inbox.at[1, rows], inbox.at[5, rows], (twin, grp))
    for part in range(2):
        add_message(0, part)
        add_message(1, part)
    for part in range(2):
        copies["half", part].wait_recv()
    for part in range(2):
        add_message(6, part)
    for part in range(2):
        copies["on_outer", part].wait_recv()
        add_message(4, part)
        copies["on_inner", part].wait_recv()
        add_message(5, part)
    for part in range(2):
        copies["far", part].wait_recv()
        add_message(3, part)

    copies["up"].wait_recv()
    copies["down"].wait_recv()
    loads[4].wait()
    loads[5].wait()
    rows = []
    for q in range(owned):
        terms = assembled_ref[q] * values[q : q + 1, :]
        rows.append(jnp.sum(terms.T, axis=0, keepdims=True))
    applied = jnp.concatenate(rows, axis=0)
    under = jnp.where(grp > 0, lower[...], 0.0)
    over = jnp.where(grp < groups - 1, upper[...], 0.0)
    product_ref[...] = applied - below[...] * under - above[...] * over
    for copy in copies.values():
        copy.wait_send()


def write_out(schur, assembled, product, schur_hbm, assembled_hbm, product_hbm, sem):
    copies = [
        pltpu.make_async_copy(source, target, sem.at[i])
        for i, (source, target) in enumerate(
            ((schur, schur_hbm.at[0, 0]), (assembled, assembled_hbm.at[0]), (product, product_hbm.at[0]))
        )
    ]
    for copy in copies:
        copy.start()
    for copy in copies:
        copy.wait()


def shards(block_map, interior_inverse, coupling, boundary_block, interface_values, below_weight, above_weight):
    size, groups = lax.axis_size("sub"), lax.axis_size("grp")
    inner = coupling.shape[2]
    count, width = boundary_block.shape[2:4]
    owned = interface_values.shape[1]
    bf16 = jnp.bfloat16
    pair = TAG + 2 * width
    results = pl.pallas_call(
        functools.partial(kernel, size, groups),
        out_shape=(
            pltpu.VMEM((count, width, width), F32),
            pltpu.VMEM((owned, width, width), F32),
            pltpu.VMEM((owned, width), F32),
        ),
        in_specs=[pl.BlockSpec(memory_space=pl.ANY)] * 7,
        out_specs=[pl.BlockSpec(memory_space=pltpu.VMEM)] * 3,
        scratch_shapes=[
            pltpu.SMEM(block_map.shape, jnp.int32),
            pltpu.VMEM((inner, inner), bf16),
            pltpu.VMEM((count, inner, width), bf16),
            pltpu.VMEM((count, width, width), bf16),
            pltpu.VMEM((owned, width), F32),
            pltpu.VMEM((owned, width), F32),
            pltpu.VMEM((owned, width), F32),
            pltpu.VMEM((owned, width), F32),
            pltpu.VMEM((owned, width), F32),
            pltpu.VMEM((pair, width), F32),
            pltpu.VMEM((TAG + width, width), F32),
            pltpu.VMEM((count, width, width), F32),
            pltpu.VMEM((7, pair, width), F32),
            pltpu.SemaphoreType.DMA((11,)),
            pltpu.SemaphoreType.DMA((16,)),
            pltpu.SemaphoreType.DMA((16,)),
            pltpu.SemaphoreType.REGULAR,
        ],
        compiler_params=pltpu.CompilerParams(
            collective_id=0, has_side_effects=True, vmem_limit_bytes=56 * 1024 * 1024
        ),
        name="condense_and_assemble",
    )(block_map, interior_inverse, coupling, boundary_block, interface_values, below_weight, above_weight)

    results = [pltpu.with_memory_space_constraint(x, pltpu.VMEM) for x in results]
    return pl.pallas_call(
        write_out,
        out_shape=(
            jax.ShapeDtypeStruct((1, 1, count, width, width), F32),
            jax.ShapeDtypeStruct((1, owned, width, width), F32),
            jax.ShapeDtypeStruct((1, owned, width), F32),
        ),
        in_specs=[pl.BlockSpec(memory_space=pltpu.VMEM)] * 3,
        out_specs=[pl.BlockSpec(memory_space=pl.ANY)] * 3,
        scratch_shapes=[pltpu.SemaphoreType.DMA((3,))],
        name="write_out",
    )(*results)


def solution(mesh):
    placed = (
        P("grp", "sub", None),
        P("grp", "sub", None, None),
        P("grp", "sub", None, None),
        P("grp", "sub", None, None, None),
        P("grp", "sub", None),
        P("grp", "sub", None),
        P("grp", "sub", None),
    )
    return jax.shard_map(
        shards,
        mesh=mesh,
        in_specs=placed,
        out_specs=(
            P("grp", "sub", None, None, None),
            P("grp", "sub", None, None),
            P("grp", "sub", None),
        ),
        check_vma=False,
    )
```

```python
import functools

import jax
import jax.numpy as jnp
from jax import lax
from jax.experimental import pallas as pl
from jax.experimental.pallas import tpu as pltpu
from jax.sharding import PartitionSpec as P

MESH = pl.DeviceIdType.MESH
F32 = jnp.float32
PLANES = 8
TAG = 8


def arrange(block_map, me, size):
    count = block_map.shape[-1]
    ids = [block_map[0, 0, k] for k in range(count)]
    half = lax.rem(me + size // 2, size)
    keys = []
    seen = jnp.int32(0)
    for block in ids:
        owner = block // 4
        is_half = owner == half
        keys.append(jnp.where(owner == me, 3, jnp.where(is_half, jnp.where(seen > 0, 1, 2), 0)))
        seen = seen + is_half.astype(jnp.int32)
    places = []
    for k in range(count):
        place = jnp.int32(0)
        for j in range(count):
            if j < k:
                place = place + (keys[j] <= keys[k]).astype(jnp.int32)
            elif j > k:
                place = place + (keys[j] < keys[k]).astype(jnp.int32)
        places.append(place)
    order, tags = [], []
    for i in range(count):
        pick, tag = jnp.int32(0), jnp.int32(0)
        for k in range(count):
            pick = pick + jnp.where(places[k] == i, k, 0)
            tag = tag + jnp.where(places[k] == i, ids[k], 0)
        order.append(pick)
        tags.append(tag)
    return places, order, tags


def kernel(
    size,
    groups,
    map_hbm,
    inverse_hbm,
    coupling_hbm,
    boundary_hbm,
    values_hbm,
    below_hbm,
    above_hbm,
    schur_ref,
    assembled_ref,
    product_ref,
    block_map,
    inverse,
    coupling,
    boundary,
    values,
    below,
    above,
    lower,
    upper,
    near,
    cross,
    held,
    inbox,
    load_sem,
    send_sem,
    recv_sem,
    ready,
):
    me, grp = lax.axis_index("sub"), lax.axis_index("grp")
    core = lax.rem(me, 2)
    step = 2 * core - 1
    twin = lax.rem(me + size - step, size)
    outer = lax.rem(me + size + 2 * step, size)
    behind = lax.rem(me + size - 2 * step, size)
    inner = lax.rem(me + size - 3 * step, size)
    beyond = lax.rem(me + size + step, size)
    half = lax.rem(me + size // 2, size)
    plane = lax.rem(me // 2, PLANES)
    bottom, top = plane == 0, plane == PLANES - 1
    odd = core == 1
    bottom_odd, bottom_even = jnp.logical_and(bottom, odd), jnp.logical_and(bottom, core == 0)
    top_odd, top_even = jnp.logical_and(top, odd), jnp.logical_and(top, core == 0)
    down, up = lax.rem(grp + groups - 1, groups), lax.rem(grp + 1, groups)

    loads = [
        pltpu.make_async_copy(source, target, load_sem.at[i])
        for i, (source, target) in enumerate(
            (
                (map_hbm, block_map),
                (inverse_hbm.at[0, 0], inverse),
                (boundary_hbm.at[0, 0], boundary),
                (values_hbm.at[0], values),
                (below_hbm.at[0], below),
                (above_hbm.at[0], above),
                *((coupling_hbm.at[0, 0, :, pl.ds(k * 128, 128)], coupling.at[k]) for k in range(5)),
            )
        )
    ]
    for load in loads:
        load.start()

    barrier = pltpu.get_barrier_semaphore()
    def signal(semaphore, *peers):
        for peer in peers:
            pl.semaphore_signal(semaphore, inc=1, device_id=peer, device_id_type=MESH)

    signal(barrier, (twin, grp), (half, grp), (me, down), (me, up))

    @pl.when(jnp.logical_not(top_odd))
    def _():
        signal(barrier, (outer, grp), (beyond, grp))

    @pl.when(jnp.logical_not(top_even))
    def _():
        signal(barrier, (behind, grp), (inner, grp))

    def describe(index, source, target, device):
        return pltpu.make_async_remote_copy(
            src_ref=source,
            dst_ref=target,
            send_sem=send_sem.at[index],
            recv_sem=recv_sem.at[index],
            device_id=device,
            device_id_type=MESH,
        )

    def send(*args):
        copy = describe(*args)
        copy.start()
        return copy

    first, second = pl.ds(0, TAG + 128), pl.ds(TAG + 128, 128)

    loads[0].wait()
    places, order, tags = arrange(block_map, me, size)

    def label(target, numbers):
        rows = lax.broadcasted_iota(jnp.int32, (TAG, 128), 0)
        target[0:TAG, :] = jnp.where(rows == 0, numbers[0], numbers[1]).astype(F32)

    label(near, tags[0:2])
    label(cross, (tags[2], tags[1]))

    for load in loads[6:]:
        load.wait()
    loads[1].wait()
    loads[2].wait()

    def condense(picks):
        blocks = [coupling[pick] for pick in picks]
        wide = jnp.concatenate(blocks, axis=1)
        sums = [None] * len(picks)
        for low, high in ((0, 512), (512, inverse.shape[0])):
            solved = jnp.dot(inverse[low:high, :], wide, preferred_element_type=F32).astype(jnp.bfloat16)
            for i, block in enumerate(blocks):
                part = lax.dot_general(
                    block[low:high],
                    solved[:, i * 128 : (i + 1) * 128],
                    (((0,), (0,)), ((), ())),
                    preferred_element_type=F32,
                )
                sums[i] = part if sums[i] is None else sums[i] + part
        return [boundary[pick].astype(F32) - total for pick, total in zip(picks, sums)]

    ahead = condense(order[0:2])
    near[TAG : TAG + 128, :] = ahead[0]
    near[TAG + 128 : TAG + 256, :] = ahead[1]

    pl.semaphore_wait(barrier, 8 - 2 * bottom.astype(jnp.int32))

    copies = {}
    for part, rows in enumerate((first, second)):
        copies["outer", part] = describe(part, near.at[rows], inbox.at[0, rows], (outer, grp))
        copies["inner", part] = describe(2 + part, near.at[rows], inbox.at[1, rows], (inner, grp))
        pl.when(jnp.logical_not(bottom_even))(copies["outer", part].start)
        pl.when(top)(copies["inner", part].start)

    @pl.when(top_odd)
    def _():
        signal(ready, (outer, grp), (beyond, grp))

    @pl.when(top_even)
    def _():
        signal(ready, (behind, grp), (inner, grp))

    copies["half", 1] = send(8, near.at[second], inbox.at[6, second], (half, grp))

    later = condense(order[2:3])
    cross[TAG : TAG + 128, :] = later[0]
    copies["half", 0] = send(11, cross, inbox.at[6, first], (half, grp))
    for part in range(2):
        pl.when(jnp.logical_not(jnp.logical_or(top, bottom_odd)))(copies["inner", part].start)
    for part, rows in enumerate((first, second)):
        copies["twin", part] = send(4 + part, near.at[rows], inbox.at[2, rows], (twin, grp))
    loads[3].wait()
    copies["up"] = send(9, values, lower, (me, up))
    copies["down"] = send(10, values, upper, (me, down))
    later += condense(order[3:5])

    @pl.when(bottom)
    def _():
        pl.semaphore_wait(ready, 2)

    for part in range(2):
        pl.when(bottom_even)(copies["outer", part].start)
        pl.when(bottom_odd)(copies["inner", part].start)
    for i, block in enumerate(ahead + later):
        held[i] = block
    for k in range(5):
        schur_ref[k] = held[places[k]]

    owned = assembled_ref.shape[0]
    base = me * owned

    def add(block, tag, start=False):
        for q in range(owned):
            term = jnp.where(tag == base + q, block, 0.0)
            assembled_ref[q] = term if start else assembled_ref[q] + term

    def add_message(slot, part):
        low = TAG + part * 128
        tag = inbox[slot, part : part + 1, :].astype(jnp.int32)
        add(inbox[slot, low : low + 128, :], tag)

    add(held[3], tags[3], start=True)
    add(held[4], tags[4])

    for part in range(2):
        copies["twin", part].wait_recv()
        add_message(2, part)
    for part, rows in enumerate((first, second)):
        copies["outer", part].wait_recv()
        copies["on_outer", part] = send(12 + part, inbox.at[0, rows], inbox.at[4, rows], (twin, grp))
        copies["far", part] = send(6 + part, inbox.at[0, rows], inbox.at[3, rows], (beyond, grp))
    for part, rows in enumerate((first, second)):
        copies["inner", part].wait_recv()
        copies["on_inner", part] = send(14 + part, inbox.at[1, rows], inbox.at[5, rows], (twin, grp))
    for part in range(2):
        add_message(0, part)
        add_message(1, part)
    for part in range(2):
        copies["half", part].wait_recv()
    for part in range(2):
        add_message(6, part)
    for part in range(2):
        copies["on_outer", part].wait_recv()
        add_message(4, part)
        copies["on_inner", part].wait_recv()
        add_message(5, part)
    for part in range(2):
        copies["far", part].wait_recv()
        add_message(3, part)

    copies["up"].wait_recv()
    copies["down"].wait_recv()
    loads[4].wait()
    loads[5].wait()
    rows = []
    for q in range(owned):
        terms = assembled_ref[q] * values[q : q + 1, :]
        rows.append(jnp.sum(terms.T, axis=0, keepdims=True))
    applied = jnp.concatenate(rows, axis=0)
    under = jnp.where(grp > 0, lower[...], 0.0)
    over = jnp.where(grp < groups - 1, upper[...], 0.0)
    product_ref[...] = applied - below[...] * under - above[...] * over
    for copy in copies.values():
        copy.wait_send()


def write_out(schur, assembled, product, schur_hbm, assembled_hbm, product_hbm, sem):
    copies = [
        pltpu.make_async_copy(source, target, sem.at[i])
        for i, (source, target) in enumerate(
            ((schur, schur_hbm.at[0, 0]), (assembled, assembled_hbm.at[0]), (product, product_hbm.at[0]))
        )
    ]
    for copy in copies:
        copy.start()
    for copy in copies:
        copy.wait()


def shards(block_map, interior_inverse, coupling, boundary_block, interface_values, below_weight, above_weight):
    size, groups = lax.axis_size("sub"), lax.axis_size("grp")
    inner = coupling.shape[2]
    count, width = boundary_block.shape[2:4]
    owned = interface_values.shape[1]
    bf16 = jnp.bfloat16
    pair = TAG + 2 * width
    results = pl.pallas_call(
        functools.partial(kernel, size, groups),
        out_shape=(
            pltpu.VMEM((count, width, width), F32),
            pltpu.VMEM((owned, width, width), F32),
            pltpu.VMEM((owned, width), F32),
        ),
        in_specs=[pl.BlockSpec(memory_space=pl.ANY)] * 7,
        out_specs=[pl.BlockSpec(memory_space=pltpu.VMEM)] * 3,
        scratch_shapes=[
            pltpu.SMEM(block_map.shape, jnp.int32),
            pltpu.VMEM((inner, inner), bf16),
            pltpu.VMEM((count, inner, width), bf16),
            pltpu.VMEM((count, width, width), bf16),
            pltpu.VMEM((owned, width), F32),
            pltpu.VMEM((owned, width), F32),
            pltpu.VMEM((owned, width), F32),
            pltpu.VMEM((owned, width), F32),
            pltpu.VMEM((owned, width), F32),
            pltpu.VMEM((pair, width), F32),
            pltpu.VMEM((TAG + width, width), F32),
            pltpu.VMEM((count, width, width), F32),
            pltpu.VMEM((7, pair, width), F32),
            pltpu.SemaphoreType.DMA((11,)),
            pltpu.SemaphoreType.DMA((16,)),
            pltpu.SemaphoreType.DMA((16,)),
            pltpu.SemaphoreType.REGULAR,
        ],
        compiler_params=pltpu.CompilerParams(
            collective_id=0, has_side_effects=True, vmem_limit_bytes=56 * 1024 * 1024
        ),
        name="condense_and_assemble",
    )(block_map, interior_inverse, coupling, boundary_block, interface_values, below_weight, above_weight)

    results = [pltpu.with_memory_space_constraint(x, pltpu.VMEM) for x in results]
    return pl.pallas_call(
        write_out,
        out_shape=(
            jax.ShapeDtypeStruct((1, 1, count, width, width), F32),
            jax.ShapeDtypeStruct((1, owned, width, width), F32),
            jax.ShapeDtypeStruct((1, owned, width), F32),
        ),
        in_specs=[pl.BlockSpec(memory_space=pltpu.VMEM)] * 3,
        out_specs=[pl.BlockSpec(memory_space=pl.ANY)] * 3,
        scratch_shapes=[pltpu.SemaphoreType.DMA((3,))],
        name="write_out",
    )(*results)


def solution(mesh):
    placed = (
        P("grp", "sub", None),
        P("grp", "sub", None, None),
        P("grp", "sub", None, None),
        P("grp", "sub", None, None, None),
        P("grp", "sub", None),
        P("grp", "sub", None),
        P("grp", "sub", None),
    )
    return jax.shard_map(
        shards,
        mesh=mesh,
        in_specs=placed,
        out_specs=(
            P("grp", "sub", None, None, None),
            P("grp", "sub", None, None),
            P("grp", "sub", None),
        ),
        check_vma=False,
    )
```

```python
import functools

import jax
import jax.numpy as jnp
from jax import lax
from jax.experimental import pallas as pl
from jax.experimental.pallas import tpu as pltpu
from jax.sharding import PartitionSpec as P

MESH = pl.DeviceIdType.MESH
F32 = jnp.float32
PLANES = 8
TAG = 8


def arrange(block_map, me, size):
    count = block_map.shape[-1]
    ids = [block_map[0, 0, k] for k in range(count)]
    half = lax.rem(me + size // 2, size)
    keys = []
    seen = jnp.int32(0)
    for block in ids:
        owner = block // 4
        is_half = owner == half
        keys.append(jnp.where(owner == me, 3, jnp.where(is_half, jnp.where(seen > 0, 1, 2), 0)))
        seen = seen + is_half.astype(jnp.int32)
    places = []
    for k in range(count):
        place = jnp.int32(0)
        for j in range(count):
            if j < k:
                place = place + (keys[j] <= keys[k]).astype(jnp.int32)
            elif j > k:
                place = place + (keys[j] < keys[k]).astype(jnp.int32)
        places.append(place)
    order, tags = [], []
    for i in range(count):
        pick, tag = jnp.int32(0), jnp.int32(0)
        for k in range(count):
            pick = pick + jnp.where(places[k] == i, k, 0)
            tag = tag + jnp.where(places[k] == i, ids[k], 0)
        order.append(pick)
        tags.append(tag)
    return places, order, tags


def kernel(
    size,
    groups,
    map_hbm,
    inverse_hbm,
    coupling_hbm,
    boundary_hbm,
    values_hbm,
    below_hbm,
    above_hbm,
    schur_ref,
    assembled_ref,
    product_ref,
    block_map,
    inverse,
    coupling,
    boundary,
    values,
    below,
    above,
    lower,
    upper,
    near,
    cross,
    held,
    inbox,
    load_sem,
    send_sem,
    recv_sem,
    ready,
):
    me, grp = lax.axis_index("sub"), lax.axis_index("grp")
    core = lax.rem(me, 2)
    step = 2 * core - 1
    twin = lax.rem(me + size - step, size)
    outer = lax.rem(me + size + 2 * step, size)
    behind = lax.rem(me + size - 2 * step, size)
    inner = lax.rem(me + size - 3 * step, size)
    beyond = lax.rem(me + size + step, size)
    half = lax.rem(me + size // 2, size)
    plane = lax.rem(me // 2, PLANES)
    bottom, top = plane == 0, plane == PLANES - 1
    odd = core == 1
    bottom_odd, bottom_even = jnp.logical_and(bottom, odd), jnp.logical_and(bottom, core == 0)
    top_odd, top_even = jnp.logical_and(top, odd), jnp.logical_and(top, core == 0)
    down, up = lax.rem(grp + groups - 1, groups), lax.rem(grp + 1, groups)

    loads = [
        pltpu.make_async_copy(source, target, load_sem.at[i])
        for i, (source, target) in enumerate(
            (
                (map_hbm, block_map),
                (inverse_hbm.at[0, 0], inverse),
                (boundary_hbm.at[0, 0], boundary),
                (values_hbm.at[0], values),
                (below_hbm.at[0], below),
                (above_hbm.at[0], above),
                *((coupling_hbm.at[0, 0, :, pl.ds(k * 128, 128)], coupling.at[k]) for k in range(5)),
            )
        )
    ]
    for load in loads:
        load.start()

    barrier = pltpu.get_barrier_semaphore()
    def signal(semaphore, *peers):
        for peer in peers:
            pl.semaphore_signal(semaphore, inc=1, device_id=peer, device_id_type=MESH)

    signal(barrier, (twin, grp), (half, grp), (me, down), (me, up))

    @pl.when(jnp.logical_not(top_odd))
    def _():
        signal(barrier, (outer, grp), (beyond, grp))

    @pl.when(jnp.logical_not(top_even))
    def _():
        signal(barrier, (behind, grp), (inner, grp))

    def describe(index, source, target, device):
        return pltpu.make_async_remote_copy(
            src_ref=source,
            dst_ref=target,
            send_sem=send_sem.at[index],
            recv_sem=recv_sem.at[index],
            device_id=device,
            device_id_type=MESH,
        )

    def send(*args):
        copy = describe(*args)
        copy.start()
        return copy

    first, second = pl.ds(0, TAG + 128), pl.ds(TAG + 128, 128)

    loads[0].wait()
    places, order, tags = arrange(block_map, me, size)

    def label(target, numbers):
        rows = lax.broadcasted_iota(jnp.int32, (TAG, 128), 0)
        target[0:TAG, :] = jnp.where(rows == 0, numbers[0], numbers[1]).astype(F32)

    label(near, tags[0:2])
    label(cross, (tags[2], tags[1]))

    for load in loads[6:]:
        load.wait()
    loads[1].wait()
    loads[2].wait()

    def condense(picks):
        blocks = [coupling[pick] for pick in picks]
        wide = jnp.concatenate(blocks, axis=1)
        sums = [None] * len(picks)
        for low, high in ((0, 512), (512, inverse.shape[0])):
            solved = jnp.dot(inverse[low:high, :], wide, preferred_element_type=F32).astype(jnp.bfloat16)
            for i, block in enumerate(blocks):
                part = lax.dot_general(
                    block[low:high],
                    solved[:, i * 128 : (i + 1) * 128],
                    (((0,), (0,)), ((), ())),
                    preferred_element_type=F32,
                )
                sums[i] = part if sums[i] is None else sums[i] + part
        return [boundary[pick].astype(F32) - total for pick, total in zip(picks, sums)]

    ahead = condense(order[0:2])
    near[TAG : TAG + 128, :] = ahead[0]
    near[TAG + 128 : TAG + 256, :] = ahead[1]

    pl.semaphore_wait(barrier, 8 - 2 * bottom.astype(jnp.int32))

    copies = {}
    for part, rows in enumerate((first, second)):
        copies["outer", part] = describe(part, near.at[rows], inbox.at[0, rows], (outer, grp))
        copies["inner", part] = describe(2 + part, near.at[rows], inbox.at[1, rows], (inner, grp))
        pl.when(jnp.logical_not(bottom_even))(copies["outer", part].start)
        pl.when(top)(copies["inner", part].start)

    @pl.when(top_odd)
    def _():
        signal(ready, (outer, grp), (beyond, grp))

    @pl.when(top_even)
    def _():
        signal(ready, (behind, grp), (inner, grp))


    later = condense(order[2:3])
    cross[TAG : TAG + 128, :] = later[0]
    copies["half", 0] = send(11, cross, inbox.at[6, first], (half, grp))
    copies["half", 1] = send(8, near.at[second], inbox.at[6, second], (half, grp))
    for part in range(2):
        pl.when(jnp.logical_not(jnp.logical_or(top, bottom_odd)))(copies["inner", part].start)
    for part, rows in enumerate((first, second)):
        copies["twin", part] = send(4 + part, near.at[rows], inbox.at[2, rows], (twin, grp))
    loads[3].wait()
    copies["up"] = send(9, values, lower, (me, up))
    copies["down"] = send(10, values, upper, (me, down))
    later += condense(order[3:5])

    @pl.when(bottom)
    def _():
        pl.semaphore_wait(ready, 2)

    for part in range(2):
        pl.when(bottom_even)(copies["outer", part].start)
        pl.when(bottom_odd)(copies["inner", part].start)
    for i, block in enumerate(ahead + later):
        held[i] = block
    for k in range(5):
        schur_ref[k] = held[places[k]]

    owned = assembled_ref.shape[0]
    base = me * owned

    def add(block, tag, start=False):
        for q in range(owned):
            term = jnp.where(tag == base + q, block, 0.0)
            assembled_ref[q] = term if start else assembled_ref[q] + term

    def add_message(slot, part):
        low = TAG + part * 128
        tag = inbox[slot, part : part + 1, :].astype(jnp.int32)
        add(inbox[slot, low : low + 128, :], tag)

    add(held[3], tags[3], start=True)
    add(held[4], tags[4])

    for part in range(2):
        copies["twin", part].wait_recv()
        add_message(2, part)
    for part, rows in enumerate((first, second)):
        copies["outer", part].wait_recv()
        copies["on_outer", part] = send(12 + part, inbox.at[0, rows], inbox.at[4, rows], (twin, grp))
        copies["far", part] = send(6 + part, inbox.at[0, rows], inbox.at[3, rows], (beyond, grp))
    for part, rows in enumerate((first, second)):
        copies["inner", part].wait_recv()
        copies["on_inner", part] = send(14 + part, inbox.at[1, rows], inbox.at[5, rows], (twin, grp))
    for part in range(2):
        add_message(0, part)
        add_message(1, part)
    for part in range(2):
        copies["half", part].wait_recv()
    for part in range(2):
        add_message(6, part)
    for part in range(2):
        copies["on_outer", part].wait_recv()
        add_message(4, part)
        copies["on_inner", part].wait_recv()
        add_message(5, part)
    for part in range(2):
        copies["far", part].wait_recv()
        add_message(3, part)

    copies["up"].wait_recv()
    copies["down"].wait_recv()
    loads[4].wait()
    loads[5].wait()
    rows = []
    for q in range(owned):
        terms = assembled_ref[q] * values[q : q + 1, :]
        rows.append(jnp.sum(terms.T, axis=0, keepdims=True))
    applied = jnp.concatenate(rows, axis=0)
    under = jnp.where(grp > 0, lower[...], 0.0)
    over = jnp.where(grp < groups - 1, upper[...], 0.0)
    product_ref[...] = applied - below[...] * under - above[...] * over
    for copy in copies.values():
        copy.wait_send()


def write_out(schur, assembled, product, schur_hbm, assembled_hbm, product_hbm, sem):
    copies = [
        pltpu.make_async_copy(source, target, sem.at[i])
        for i, (source, target) in enumerate(
            ((schur, schur_hbm.at[0, 0]), (assembled, assembled_hbm.at[0]), (product, product_hbm.at[0]))
        )
    ]
    for copy in copies:
        copy.start()
    for copy in copies:
        copy.wait()


def shards(block_map, interior_inverse, coupling, boundary_block, interface_values, below_weight, above_weight):
    size, groups = lax.axis_size("sub"), lax.axis_size("grp")
    inner = coupling.shape[2]
    count, width = boundary_block.shape[2:4]
    owned = interface_values.shape[1]
    bf16 = jnp.bfloat16
    pair = TAG + 2 * width
    results = pl.pallas_call(
        functools.partial(kernel, size, groups),
        out_shape=(
            pltpu.VMEM((count, width, width), F32),
            pltpu.VMEM((owned, width, width), F32),
            pltpu.VMEM((owned, width), F32),
        ),
        in_specs=[pl.BlockSpec(memory_space=pl.ANY)] * 7,
        out_specs=[pl.BlockSpec(memory_space=pltpu.VMEM)] * 3,
        scratch_shapes=[
            pltpu.SMEM(block_map.shape, jnp.int32),
            pltpu.VMEM((inner, inner), bf16),
            pltpu.VMEM((count, inner, width), bf16),
            pltpu.VMEM((count, width, width), bf16),
            pltpu.VMEM((owned, width), F32),
            pltpu.VMEM((owned, width), F32),
            pltpu.VMEM((owned, width), F32),
            pltpu.VMEM((owned, width), F32),
            pltpu.VMEM((owned, width), F32),
            pltpu.VMEM((pair, width), F32),
            pltpu.VMEM((TAG + width, width), F32),
            pltpu.VMEM((count, width, width), F32),
            pltpu.VMEM((7, pair, width), F32),
            pltpu.SemaphoreType.DMA((11,)),
            pltpu.SemaphoreType.DMA((16,)),
            pltpu.SemaphoreType.DMA((16,)),
            pltpu.SemaphoreType.REGULAR,
        ],
        compiler_params=pltpu.CompilerParams(
            collective_id=0, has_side_effects=True, vmem_limit_bytes=56 * 1024 * 1024
        ),
        name="condense_and_assemble",
    )(block_map, interior_inverse, coupling, boundary_block, interface_values, below_weight, above_weight)

    results = [pltpu.with_memory_space_constraint(x, pltpu.VMEM) for x in results]
    return pl.pallas_call(
        write_out,
        out_shape=(
            jax.ShapeDtypeStruct((1, 1, count, width, width), F32),
            jax.ShapeDtypeStruct((1, owned, width, width), F32),
            jax.ShapeDtypeStruct((1, owned, width), F32),
        ),
        in_specs=[pl.BlockSpec(memory_space=pltpu.VMEM)] * 3,
        out_specs=[pl.BlockSpec(memory_space=pl.ANY)] * 3,
        scratch_shapes=[pltpu.SemaphoreType.DMA((3,))],
        name="write_out",
    )(*results)


def solution(mesh):
    placed = (
        P("grp", "sub", None),
        P("grp", "sub", None, None),
        P("grp", "sub", None, None),
        P("grp", "sub", None, None, None),
        P("grp", "sub", None),
        P("grp", "sub", None),
        P("grp", "sub", None),
    )
    return jax.shard_map(
        shards,
        mesh=mesh,
        in_specs=placed,
        out_specs=(
            P("grp", "sub", None, None, None),
            P("grp", "sub", None, None),
            P("grp", "sub", None),
        ),
        check_vma=False,
    )
```

```python
import functools

import jax
import jax.numpy as jnp
from jax import lax
from jax.experimental import pallas as pl
from jax.experimental.pallas import tpu as pltpu
from jax.sharding import PartitionSpec as P

MESH = pl.DeviceIdType.MESH
F32 = jnp.float32
PLANES = 8
TAG = 8


def arrange(block_map, me, size):
    count = block_map.shape[-1]
    ids = [block_map[0, 0, k] for k in range(count)]
    half = lax.rem(me + size // 2, size)
    keys = []
    seen = jnp.int32(0)
    for block in ids:
        owner = block // 4
        is_half = owner == half
        keys.append(jnp.where(owner == me, 3, jnp.where(is_half, jnp.where(seen > 0, 1, 2), 0)))
        seen = seen + is_half.astype(jnp.int32)
    places = []
    for k in range(count):
        place = jnp.int32(0)
        for j in range(count):
            if j < k:
                place = place + (keys[j] <= keys[k]).astype(jnp.int32)
            elif j > k:
                place = place + (keys[j] < keys[k]).astype(jnp.int32)
        places.append(place)
    order, tags = [], []
    for i in range(count):
        pick, tag = jnp.int32(0), jnp.int32(0)
        for k in range(count):
            pick = pick + jnp.where(places[k] == i, k, 0)
            tag = tag + jnp.where(places[k] == i, ids[k], 0)
        order.append(pick)
        tags.append(tag)
    return places, order, tags


def kernel(
    size,
    groups,
    map_hbm,
    inverse_hbm,
    coupling_hbm,
    boundary_hbm,
    values_hbm,
    below_hbm,
    above_hbm,
    schur_ref,
    assembled_ref,
    product_ref,
    block_map,
    inverse,
    coupling,
    boundary,
    values,
    below,
    above,
    lower,
    upper,
    near,
    cross,
    held,
    inbox,
    load_sem,
    send_sem,
    recv_sem,
    ready,
):
    me, grp = lax.axis_index("sub"), lax.axis_index("grp")
    core = lax.rem(me, 2)
    step = 2 * core - 1
    twin = lax.rem(me + size - step, size)
    outer = lax.rem(me + size + 2 * step, size)
    behind = lax.rem(me + size - 2 * step, size)
    inner = lax.rem(me + size - 3 * step, size)
    beyond = lax.rem(me + size + step, size)
    half = lax.rem(me + size // 2, size)
    plane = lax.rem(me // 2, PLANES)
    bottom, top = plane == 0, plane == PLANES - 1
    odd = core == 1
    bottom_odd, bottom_even = jnp.logical_and(bottom, odd), jnp.logical_and(bottom, core == 0)
    top_odd, top_even = jnp.logical_and(top, odd), jnp.logical_and(top, core == 0)
    down, up = lax.rem(grp + groups - 1, groups), lax.rem(grp + 1, groups)

    loads = [
        pltpu.make_async_copy(source, target, load_sem.at[i])
        for i, (source, target) in enumerate(
            (
                (map_hbm, block_map),
                (inverse_hbm.at[0, 0], inverse),
                (boundary_hbm.at[0, 0], boundary),
                (values_hbm.at[0], values),
                (below_hbm.at[0], below),
                (above_hbm.at[0], above),
                *((coupling_hbm.at[0, 0, :, pl.ds(k * 128, 128)], coupling.at[k]) for k in range(5)),
            )
        )
    ]
    for load in loads[:2] + loads[6:] + loads[2:6]:
        load.start()

    barrier = pltpu.get_barrier_semaphore()
    def signal(semaphore, *peers):
        for peer in peers:
            pl.semaphore_signal(semaphore, inc=1, device_id=peer, device_id_type=MESH)

    signal(barrier, (twin, grp), (half, grp), (me, down), (me, up))

    @pl.when(jnp.logical_not(top_odd))
    def _():
        signal(barrier, (outer, grp), (beyond, grp))

    @pl.when(jnp.logical_not(top_even))
    def _():
        signal(barrier, (behind, grp), (inner, grp))

    def describe(index, source, target, device):
        return pltpu.make_async_remote_copy(
            src_ref=source,
            dst_ref=target,
            send_sem=send_sem.at[index],
            recv_sem=recv_sem.at[index],
            device_id=device,
            device_id_type=MESH,
        )

    def send(*args):
        copy = describe(*args)
        copy.start()
        return copy

    first, second = pl.ds(0, TAG + 128), pl.ds(TAG + 128, 128)

    loads[0].wait()
    places, order, tags = arrange(block_map, me, size)

    def label(target, numbers):
        rows = lax.broadcasted_iota(jnp.int32, (TAG, 128), 0)
        target[0:TAG, :] = jnp.where(rows == 0, numbers[0], numbers[1]).astype(F32)

    label(near, tags[0:2])
    label(cross, (tags[2], tags[1]))

    for load in loads[6:]:
        load.wait()
    loads[1].wait()
    loads[2].wait()

    def condense(picks):
        blocks = [coupling[pick] for pick in picks]
        wide = jnp.concatenate(blocks, axis=1)
        sums = [None] * len(picks)
        for low, high in ((0, 512), (512, inverse.shape[0])):
            solved = jnp.dot(inverse[low:high, :], wide, preferred_element_type=F32).astype(jnp.bfloat16)
            for i, block in enumerate(blocks):
                part = lax.dot_general(
                    block[low:high],
                    solved[:, i * 128 : (i + 1) * 128],
                    (((0,), (0,)), ((), ())),
                    preferred_element_type=F32,
                )
                sums[i] = part if sums[i] is None else sums[i] + part
        return [boundary[pick].astype(F32) - total for pick, total in zip(picks, sums)]

    ahead = condense(order[0:2])
    near[TAG : TAG + 128, :] = ahead[0]
    near[TAG + 128 : TAG + 256, :] = ahead[1]

    pl.semaphore_wait(barrier, 8 - 2 * bottom.astype(jnp.int32))

    copies = {}
    for part, rows in enumerate((first, second)):
        copies["outer", part] = describe(part, near.at[rows], inbox.at[0, rows], (outer, grp))
        copies["inner", part] = describe(2 + part, near.at[rows], inbox.at[1, rows], (inner, grp))
        pl.when(jnp.logical_not(bottom_even))(copies["outer", part].start)
        pl.when(top)(copies["inner", part].start)

    @pl.when(top_odd)
    def _():
        signal(ready, (outer, grp), (beyond, grp))

    @pl.when(top_even)
    def _():
        signal(ready, (behind, grp), (inner, grp))

    copies["half", 1] = send(8, near.at[second], inbox.at[6, second], (half, grp))

    later = condense(order[2:3])
    cross[TAG : TAG + 128, :] = later[0]
    copies["half", 0] = send(11, cross, inbox.at[6, first], (half, grp))
    for part in range(2):
        pl.when(jnp.logical_not(jnp.logical_or(top, bottom_odd)))(copies["inner", part].start)
    for part, rows in enumerate((first, second)):
        copies["twin", part] = send(4 + part, near.at[rows], inbox.at[2, rows], (twin, grp))
    loads[3].wait()
    copies["up"] = send(9, values, lower, (me, up))
    copies["down"] = send(10, values, upper, (me, down))
    later += condense(order[3:5])

    @pl.when(bottom)
    def _():
        pl.semaphore_wait(ready, 2)

    for part in range(2):
        pl.when(bottom_even)(copies["outer", part].start)
        pl.when(bottom_odd)(copies["inner", part].start)
    for i, block in enumerate(ahead + later):
        held[i] = block
    for k in range(5):
        schur_ref[k] = held[places[k]]

    owned = assembled_ref.shape[0]
    base = me * owned

    def add(block, tag, start=False):
        for q in range(owned):
            term = jnp.where(tag == base + q, block, 0.0)
            assembled_ref[q] = term if start else assembled_ref[q] + term

    def add_message(slot, part):
        low = TAG + part * 128
        tag = inbox[slot, part : part + 1, :].astype(jnp.int32)
        add(inbox[slot, low : low + 128, :], tag)

    add(held[3], tags[3], start=True)
    add(held[4], tags[4])

    for part in range(2):
        copies["twin", part].wait_recv()
        add_message(2, part)
    for part, rows in enumerate((first, second)):
        copies["outer", part].wait_recv()
        copies["on_outer", part] = send(12 + part, inbox.at[0, rows], inbox.at[4, rows], (twin, grp))
        copies["far", part] = send(6 + part, inbox.at[0, rows], inbox.at[3, rows], (beyond, grp))
    for part, rows in enumerate((first, second)):
        copies["inner", part].wait_recv()
        copies["on_inner", part] = send(14 + part, inbox.at[1, rows], inbox.at[5, rows], (twin, grp))
    for part in range(2):
        add_message(0, part)
        add_message(1, part)
    for part in range(2):
        copies["half", part].wait_recv()
    for part in range(2):
        add_message(6, part)
    for part in range(2):
        copies["on_outer", part].wait_recv()
        add_message(4, part)
        copies["on_inner", part].wait_recv()
        add_message(5, part)
    for part in range(2):
        copies["far", part].wait_recv()
        add_message(3, part)

    copies["up"].wait_recv()
    copies["down"].wait_recv()
    loads[4].wait()
    loads[5].wait()
    rows = []
    for q in range(owned):
        terms = assembled_ref[q] * values[q : q + 1, :]
        rows.append(jnp.sum(terms.T, axis=0, keepdims=True))
    applied = jnp.concatenate(rows, axis=0)
    under = jnp.where(grp > 0, lower[...], 0.0)
    over = jnp.where(grp < groups - 1, upper[...], 0.0)
    product_ref[...] = applied - below[...] * under - above[...] * over
    for copy in copies.values():
        copy.wait_send()


def write_out(schur, assembled, product, schur_hbm, assembled_hbm, product_hbm, sem):
    copies = [
        pltpu.make_async_copy(source, target, sem.at[i])
        for i, (source, target) in enumerate(
            ((schur, schur_hbm.at[0, 0]), (assembled, assembled_hbm.at[0]), (product, product_hbm.at[0]))
        )
    ]
    for copy in copies:
        copy.start()
    for copy in copies:
        copy.wait()


def shards(block_map, interior_inverse, coupling, boundary_block, interface_values, below_weight, above_weight):
    size, groups = lax.axis_size("sub"), lax.axis_size("grp")
    inner = coupling.shape[2]
    count, width = boundary_block.shape[2:4]
    owned = interface_values.shape[1]
    bf16 = jnp.bfloat16
    pair = TAG + 2 * width
    results = pl.pallas_call(
        functools.partial(kernel, size, groups),
        out_shape=(
            pltpu.VMEM((count, width, width), F32),
            pltpu.VMEM((owned, width, width), F32),
            pltpu.VMEM((owned, width), F32),
        ),
        in_specs=[pl.BlockSpec(memory_space=pl.ANY)] * 7,
        out_specs=[pl.BlockSpec(memory_space=pltpu.VMEM)] * 3,
        scratch_shapes=[
            pltpu.SMEM(block_map.shape, jnp.int32),
            pltpu.VMEM((inner, inner), bf16),
            pltpu.VMEM((count, inner, width), bf16),
            pltpu.VMEM((count, width, width), bf16),
            pltpu.VMEM((owned, width), F32),
            pltpu.VMEM((owned, width), F32),
            pltpu.VMEM((owned, width), F32),
            pltpu.VMEM((owned, width), F32),
            pltpu.VMEM((owned, width), F32),
            pltpu.VMEM((pair, width), F32),
            pltpu.VMEM((TAG + width, width), F32),
            pltpu.VMEM((count, width, width), F32),
            pltpu.VMEM((7, pair, width), F32),
            pltpu.SemaphoreType.DMA((11,)),
            pltpu.SemaphoreType.DMA((16,)),
            pltpu.SemaphoreType.DMA((16,)),
            pltpu.SemaphoreType.REGULAR,
        ],
        compiler_params=pltpu.CompilerParams(
            collective_id=0, has_side_effects=True, vmem_limit_bytes=56 * 1024 * 1024
        ),
        name="condense_and_assemble",
    )(block_map, interior_inverse, coupling, boundary_block, interface_values, below_weight, above_weight)

    results = [pltpu.with_memory_space_constraint(x, pltpu.VMEM) for x in results]
    return pl.pallas_call(
        write_out,
        out_shape=(
            jax.ShapeDtypeStruct((1, 1, count, width, width), F32),
            jax.ShapeDtypeStruct((1, owned, width, width), F32),
            jax.ShapeDtypeStruct((1, owned, width), F32),
        ),
        in_specs=[pl.BlockSpec(memory_space=pltpu.VMEM)] * 3,
        out_specs=[pl.BlockSpec(memory_space=pl.ANY)] * 3,
        scratch_shapes=[pltpu.SemaphoreType.DMA((3,))],
        name="write_out",
    )(*results)


def solution(mesh):
    placed = (
        P("grp", "sub", None),
        P("grp", "sub", None, None),
        P("grp", "sub", None, None),
        P("grp", "sub", None, None, None),
        P("grp", "sub", None),
        P("grp", "sub", None),
        P("grp", "sub", None),
    )
    return jax.shard_map(
        shards,
        mesh=mesh,
        in_specs=placed,
        out_specs=(
            P("grp", "sub", None, None, None),
            P("grp", "sub", None, None),
            P("grp", "sub", None),
        ),
        check_vma=False,
    )
```
